32 devices in a mesh: blk: 32 (over z, y, x, core), grp: 1.
Axes of the slice: x: 2, y: 2, z: 4, core: 2. Of those that a mesh axis runs over, the one named last changes fastest.
Arguments:
- fields: float32 [3, 768, 32, 256], P(None, 'blk', 'grp'), may hold values from -100 to 100
- mask: int32 [32, 256], P('grp'), may hold values from 0 to 1, as said below
Outputs:
- r_factor: float32 [768, 768], replicated
- active_force: float32 [2, 768, 32, 256], P(None, 'blk', 'grp')
The draws below stay inside these ranges and needn't reach their ends.
Inputs may be any that keep to these rules, and one draw needn't show every extreme that they name: `mask`: grid rows k * 32 to (k + 1) * 32 - 1, for each k, hold exactly 4352 fluid points together.
All inputs are finite; a program needn't handle non-finite values.
Results may differ from the reference program's by a relative error of at most 0.0003.
Values sent between devices are 32-bit elements; how exact they have to be, the bound alone decides.
A program may use at most 256 MiB of HBM per device.

```python
import math
import jax
import jax.numpy as jnp
from jax import lax

NY = 256
T_SIZE = 768
NX = 32
N_BLK = 32
N_GRP = 1


def draw_fields(key, part):
    row_scale = jnp.exp(jax.random.uniform(jax.random.fold_in(key, 1), (NX,), jnp.float32, 0.0, math.log(30.0)))
    col_scale = jnp.exp(jax.random.uniform(jax.random.fold_in(key, 2), (NY,), jnp.float32, 0.0, math.log(3.0)))
    amplitude = jax.random.uniform(jax.random.fold_in(key, 3), (T_SIZE,), jnp.float32, 0.4, 1.6)
    common = jnp.clip(jax.random.normal(jax.random.fold_in(key, 4), (3, NX, NY), jnp.float32), -4.0, 4.0)
    varying = jnp.clip(jax.random.normal(jax.random.fold_in(key, 5), (3, T_SIZE, NX, NY), jnp.float32), -4.0, 4.0)
    values = 0.6 * common[:, None] + amplitude[None, :, None, None] * varying
    values = values * row_scale[None, None, :, None] * col_scale[None, None, None, :]
    return (values / 8.0).astype(jnp.float32)


def draw_mask(key, part):
    positions = jnp.arange(N_BLK, dtype=jnp.int32)
    lengths = NY // N_BLK * (positions - positions % 2)
    group_keys = jax.random.split(jax.random.fold_in(key, 11), N_GRP)
    shuffled = jax.vmap(lambda group_key: jax.random.permutation(group_key, lengths))(group_keys).reshape(NX)
    starts = jax.random.randint(jax.random.fold_in(key, 12), (NX,), 0, NY)
    columns = jnp.arange(NY, dtype=jnp.int32)
    offsets = (columns[None, :] - starts[:, None]) % NY
    return (offsets >= shuffled[:, None]).astype(jnp.int32)


def setup_inputs(seed: int = 0) -> dict:
    keys = jax.random.split(jax.random.key(seed), 3)
    return {
        "fields": draw_fields(jax.random.fold_in(keys[2], 71), 0),
        "mask": draw_mask(jax.random.fold_in(keys[2], 71), 0),
    }


def slope_rows(values):
    return 0.5 * (jnp.roll(values, -1, 1) - jnp.roll(values, 1, 1))

def slope_cols(values):
    return 0.5 * (jnp.roll(values, -1, 2) - jnp.roll(values, 1, 2))

def reference(fields, mask):
    q_first = fields[1]
    q_second = fields[2]
    force_x = slope_rows(q_first) + slope_cols(q_second)
    force_y = slope_rows(q_second) - slope_cols(q_first)
    active_force = jnp.stack([force_x, force_y])
    weights = mask.astype(jnp.float32)

    def accumulate(block_index, gram_matrix):
        first_row = (block_index * N_BLK).astype(jnp.int32)
        field_block = lax.dynamic_slice_in_dim(fields, first_row, N_BLK, 2)
        force_block = lax.dynamic_slice_in_dim(active_force, first_row, N_BLK, 2)
        mask_block = lax.dynamic_slice_in_dim(weights, first_row, N_BLK, 0)
        stacked = jnp.concatenate([field_block, force_block], 0) * mask_block[None, None]
        return gram_matrix + jnp.einsum('ftrc,fsrc->ts', stacked, stacked, precision=lax.Precision.HIGHEST)
    gram_matrix = lax.fori_loop(jnp.int32(0), jnp.int32(N_GRP), accumulate, jnp.zeros((T_SIZE, T_SIZE), jnp.float32))
    gram_matrix = gram_matrix / float(NX * NY)
    r_factor = jnp.linalg.cholesky(gram_matrix).T
    return (r_factor, active_force)
```

```python
import functools
import jax
import jax.numpy as jnp
from jax import lax
from jax.experimental import pallas as pl
from jax.experimental.pallas import tpu as pltpu
from jax.sharding import PartitionSpec as P

NB = 128
HIGHEST = lax.Precision.HIGHEST
MESH_ID = pl.DeviceIdType.MESH


def tiles(size):
    n = size // NB
    return [(i, j) for i in range(n) for j in range(i, n)]


def packed_rows(size, count):
    unit = 8 * count
    return -(-len(tiles(size)) * NB // unit) * unit


def stages(count):
    return [(1, 2), (2, 4), (8, count // 8)]


def sum_kernel(count, g_ref, full, acc, buf0, buf1, buf2, send, recv, gsend, grecv):
    me = lax.axis_index("blk")
    plan = stages(count)
    bufs = [buf0, buf1, buf2]

    def peer(stride, size, step):
        here = (me // stride) % size
        there = (here + step) % size
        return there, me + (there - here) * stride

    barrier = pltpu.get_barrier_semaphore()
    greeted = 0
    for stride, size in plan:
        for step in range(1, size):
            pl.semaphore_signal(barrier, inc=1, device_id={"blk": peer(stride, size, step)[1]}, device_id_type=MESH_ID)
            greeted += 1
    for b, (i, j) in enumerate(tiles(g_ref.shape[0])):
        acc[b * NB:(b + 1) * NB, :] = g_ref[i * NB:(i + 1) * NB, j * NB:(j + 1) * NB]
    used = len(tiles(g_ref.shape[0])) * NB
    total = acc.shape[0]
    if used < total:
        acc[used:, :] = jnp.zeros((total - used, NB), jnp.float32)
    pl.semaphore_wait(barrier, greeted)

    started = []
    base = 0
    length = total
    slot = 0
    owned = []
    for (stride, size), buf in zip(plan, bufs):
        length = length // size
        here = (me // stride) % size
        wave = []
        for step in range(1, size):
            there, device = peer(stride, size, step)
            copy = pltpu.make_async_remote_copy(
                src_ref=acc.at[pl.ds(pl.multiple_of(base + there * length, 8), length)],
                dst_ref=buf.at[step - 1],
                send_sem=send.at[slot], recv_sem=recv.at[slot],
                device_id={"blk": device}, device_id_type=MESH_ID)
            copy.start()
            wave.append(copy)
            slot += 1
        base = pl.multiple_of(base + here * length, 8)
        value = acc[pl.ds(base, length), :]
        for step, copy in enumerate(wave):
            copy.wait_recv()
            value = value + buf[step]
        acc[pl.ds(base, length), :] = value
        owned.append((base, length))
        started += wave
    full[pl.ds(base, length), :] = acc[pl.ds(base, length), :]
    slot = 0
    for (stride, size), (base, length) in reversed(list(zip(plan, owned))):
        piece = pl.ds(base, length)
        wave = []
        for step in range(1, size):
            copy = pltpu.make_async_remote_copy(
                src_ref=full.at[piece], dst_ref=full.at[piece],
                send_sem=gsend.at[slot], recv_sem=grecv.at[slot],
                device_id={"blk": peer(stride, size, step)[1]}, device_id_type=MESH_ID)
            copy.start()
            wave.append(copy)
            slot += 1
        for copy in wave:
            copy.wait_recv()
        started += wave
    for copy in started:
        copy.wait_send()


def summed(gram):
    count = lax.axis_size("blk")
    size = gram.shape[0]
    total = packed_rows(size, count)
    plan = stages(count)
    lengths = [total // 2, total // 8, total // count]
    copies = sum(s - 1 for _, s in plan)
    return pl.pallas_call(
        functools.partial(sum_kernel, count),
        out_shape=jax.ShapeDtypeStruct((total, NB), jnp.float32),
        in_specs=[pl.BlockSpec(memory_space=pltpu.VMEM)],
        out_specs=pl.BlockSpec(memory_space=pltpu.VMEM),
        scratch_shapes=[pltpu.VMEM((total, NB), jnp.float32)]
        + [pltpu.VMEM((s - 1, rows, NB), jnp.float32) for (_, s), rows in zip(plan, lengths)]
        + [pltpu.SemaphoreType.DMA((copies,))] * 4,
        compiler_params=pltpu.CompilerParams(collective_id=0, has_side_effects=True, vmem_limit_bytes=56 * 2**20),
    )(gram)


def factor(work, j, u_ref, z_ref):
    base = pl.multiple_of(j * NB, NB)
    D = [work[pl.ds(base + 8 * i, 8), pl.ds(base, NB)] for i in range(16)]
    rows = lax.broadcasted_iota(jnp.int32, (8, NB), 0)
    lanes = lax.broadcasted_iota(jnp.int32, (8, NB), 1)
    Z = [jnp.where(rows + 8 * i == lanes, 1.0, 0.0).astype(jnp.float32) for i in range(16)]
    full = lambda x: jnp.broadcast_to(x, (8, NB))
    for t in range(16):
        C = [full(D[t][:, 8 * t + c:8 * t + c + 1]) for c in range(8)]
        X, Y = D[t], Z[t]
        for s in range(8):
            piv = full(C[s][s:s + 1])
            rs = lax.rsqrt(piv)
            xr, yr = full(X[s:s + 1]) * rs, full(Y[s:s + 1]) * rs
            u_ref[8 * t + s:8 * t + s + 1, :] = xr[s:s + 1]
            z_ref[8 * t + s:8 * t + s + 1, :] = yr[s:s + 1]
            inv = rs * rs
            mult = C[s] * inv
            X0, Y0 = full(X[s:s + 1]), full(Y[s:s + 1])
            X = jnp.where(rows == s, X0 * inv, X - mult * X0)
            Y = jnp.where(rows == s, Y0 * inv, Y - mult * Y0)
            for c in range(s + 1, 8):
                c0 = full(C[c][s:s + 1])
                C[c] = jnp.where(rows == s, c0 * inv, C[c] - mult * c0)
        for i in range(t + 1, 16):
            d, z = D[i], Z[i]
            cols = [full(D[i][:, 8 * t + c:8 * t + c + 1]) for c in range(8)]
            for c in range(8):
                d = d - cols[c] * full(X[c:c + 1])
                z = z - cols[c] * full(Y[c:c + 1])
            D[i], Z[i] = d, z


def chol_kernel(scale, g_ref, r_ref, work, u_ref, z_ref):
    size = work.shape[0]
    n = size // NB
    for b, (i, j) in enumerate(tiles(size)):
        work[i * NB:(i + 1) * NB, j * NB:(j + 1) * NB] = g_ref[b * NB:(b + 1) * NB, :] * scale
    for i in range(1, n):
        r_ref[i * NB:(i + 1) * NB, :i * NB] = jnp.zeros((NB, i * NB), jnp.float32)
    tri = lax.broadcasted_iota(jnp.int32, (NB, NB), 0) <= lax.broadcasted_iota(jnp.int32, (NB, NB), 1)

    @pl.loop(0, n)
    def _(j):
        factor(work, j, u_ref, z_ref)
        for jj in range(n):
            @pl.when(j == jj)
            def _(jj=jj):
                lo, hi = jj * NB, (jj + 1) * NB
                r_ref[lo:hi, lo:hi] = jnp.where(tri, u_ref[...], 0.0)
                if jj < n - 1:
                    panel = jnp.dot(z_ref[...], work[lo:hi, hi:], precision=HIGHEST, preferred_element_type=jnp.float32)
                    r_ref[lo:hi, hi:] = panel
                    step = 2 * NB
                    for a in range(hi, size, step):
                        b = min(a + step, size)
                        strip = lax.dot_general(r_ref[lo:hi, a:b], r_ref[lo:hi, a:], (((0,), (0,)), ((), ())), precision=HIGHEST, preferred_element_type=jnp.float32)
                        work[a:b, a:] = work[a:b, a:] - strip


def factored(packed, size, scale):
    return pl.pallas_call(
        functools.partial(chol_kernel, scale),
        out_shape=jax.ShapeDtypeStruct((size, size), jnp.float32),
        in_specs=[pl.BlockSpec(memory_space=pltpu.VMEM)],
        out_specs=pl.BlockSpec(memory_space=pltpu.VMEM),
        scratch_shapes=[pltpu.VMEM((size, size), jnp.float32), pltpu.VMEM((NB, NB), jnp.float32), pltpu.VMEM((NB, NB), jnp.float32)],
        compiler_params=pltpu.CompilerParams(vmem_limit_bytes=56 * 2**20),
    )(packed)


def padded(cells, sides, width):
    for axis, dim in sides:
        count = lax.axis_size(axis)
        head = lax.slice_in_dim(cells, 0, width, axis=dim)
        tail = lax.slice_in_dim(cells, cells.shape[dim] - width, cells.shape[dim], axis=dim)
        cells = jnp.concatenate(
            [
                lax.ppermute(tail, axis, [(i, (i + 1) % count) for i in range(count)]),
                cells,
                lax.ppermute(head, axis, [((i + 1) % count, i) for i in range(count)]),
            ],
            axis=dim,
        )
    return cells


def pair_gram(left_block, right_block):
    return jnp.einsum("ftm,fsm->ts", left_block, right_block, precision=lax.Precision.HIGH)


def per_device(fields, mask):
    widened = padded(fields[1:3], (("grp", 2),), 1)
    middle = widened[:, :, 1:-1]
    slope_rows = 0.5 * (widened[:, :, 2:] - widened[:, :, :-2])
    slope_cols = 0.5 * (jnp.roll(middle, -1, 3) - jnp.roll(middle, 1, 3))
    active_force = jnp.stack([slope_rows[0] + slope_cols[1], slope_rows[1] - slope_cols[0]])
    stacked = jnp.concatenate([fields, active_force], 0)
    groups = lax.axis_size("grp")
    rows_here, columns = mask.shape
    weighted = stacked * mask.astype(jnp.float32)[None, None]
    relaid = lax.all_to_all(weighted, "blk", split_axis=2, concat_axis=1, tiled=True)
    snapshots = relaid.reshape(relaid.shape[0], relaid.shape[1], -1)
    packed = summed(pair_gram(snapshots, snapshots))
    if groups > 1:
        packed = lax.psum(packed, "grp")
    r_factor = factored(packed, snapshots.shape[1], 1.0 / float(rows_here * groups * columns))
    return (r_factor, active_force)


def solution(mesh):
    placed = (P(None, "blk", "grp", None), P("grp", None))
    return jax.shard_map(
        per_device,
        mesh=mesh,
        in_specs=placed,
        out_specs=(P(), P(None, "blk", "grp", None)),
        check_vma=False,
    )
```

```python
import functools
import jax
import jax.numpy as jnp
from jax import lax
from jax.experimental import pallas as pl
from jax.experimental.pallas import tpu as pltpu
from jax.sharding import PartitionSpec as P

NB = 128
HIGHEST = lax.Precision.HIGHEST
MESH_ID = pl.DeviceIdType.MESH


def tiles(size):
    n = size // NB
    return [(i, j) for i in range(n) for j in range(i, n)]


def packed_rows(size, count):
    unit = 8 * count
    return -(-len(tiles(size)) * NB // unit) * unit


def stages(count):
    return [(1, 2), (2, 4), (8, count // 8)]


def sum_kernel(count, g_ref, full, acc, buf0, buf1, buf2, send, recv, gsend, grecv):
    me = lax.axis_index("blk")
    plan = stages(count)
    bufs = [buf0, buf1, buf2]

    def peer(stride, size, step):
        here = (me // stride) % size
        there = (here + step) % size
        return there, me + (there - here) * stride

    barrier = pltpu.get_barrier_semaphore()
    greeted = 0
    for stride, size in plan:
        for step in range(1, size):
            pl.semaphore_signal(barrier, inc=1, device_id={"blk": peer(stride, size, step)[1]}, device_id_type=MESH_ID)
            greeted += 1
    for b, (i, j) in enumerate(tiles(g_ref.shape[0])):
        acc[b * NB:(b + 1) * NB, :] = g_ref[i * NB:(i + 1) * NB, j * NB:(j + 1) * NB]
    used = len(tiles(g_ref.shape[0])) * NB
    total = acc.shape[0]
    if used < total:
        acc[used:, :] = jnp.zeros((total - used, NB), jnp.float32)
    pl.semaphore_wait(barrier, greeted)

    started = []
    base = 0
    length = total
    slot = 0
    owned = []
    for (stride, size), buf in zip(plan, bufs):
        length = length // size
        here = (me // stride) % size
        wave = []
        for step in range(1, size):
            there, device = peer(stride, size, step)
            copy = pltpu.make_async_remote_copy(
                src_ref=acc.at[pl.ds(pl.multiple_of(base + there * length, 8), length)],
                dst_ref=buf.at[step - 1],
                send_sem=send.at[slot], recv_sem=recv.at[slot],
                device_id={"blk": device}, device_id_type=MESH_ID)
            copy.start()
            wave.append(copy)
            slot += 1
        base = pl.multiple_of(base + here * length, 8)
        value = acc[pl.ds(base, length), :]
        for step, copy in enumerate(wave):
            copy.wait_recv()
            value = value + buf[step]
        acc[pl.ds(base, length), :] = value
        owned.append((base, length))
        started += wave
    full[pl.ds(base, length), :] = acc[pl.ds(base, length), :]
    slot = 0
    for (stride, size), (base, length) in reversed(list(zip(plan, owned))):
        piece = pl.ds(base, length)
        wave = []
        for step in range(1, size):
            copy = pltpu.make_async_remote_copy(
                src_ref=full.at[piece], dst_ref=full.at[piece],
                send_sem=gsend.at[slot], recv_sem=grecv.at[slot],
                device_id={"blk": peer(stride, size, step)[1]}, device_id_type=MESH_ID)
            copy.start()
            wave.append(copy)
            slot += 1
        for copy in wave:
            copy.wait_recv()
        started += wave
    for copy in started:
        copy.wait_send()


def summed(gram):
    count = lax.axis_size("blk")
    size = gram.shape[0]
    total = packed_rows(size, count)
    plan = stages(count)
    lengths = [total // 2, total // 8, total // count]
    copies = sum(s - 1 for _, s in plan)
    return pl.pallas_call(
        functools.partial(sum_kernel, count),
        out_shape=jax.ShapeDtypeStruct((total, NB), jnp.float32),
        in_specs=[pl.BlockSpec(memory_space=pltpu.VMEM)],
        out_specs=pl.BlockSpec(memory_space=pltpu.VMEM),
        scratch_shapes=[pltpu.VMEM((total, NB), jnp.float32)]
        + [pltpu.VMEM((s - 1, rows, NB), jnp.float32) for (_, s), rows in zip(plan, lengths)]
        + [pltpu.SemaphoreType.DMA((copies,))] * 4,
        compiler_params=pltpu.CompilerParams(collective_id=0, has_side_effects=True, vmem_limit_bytes=56 * 2**20),
    )(gram)


def factor(work, j, u_ref, z_ref):
    base = pl.multiple_of(j * NB, NB)
    D = [work[pl.ds(base + 8 * i, 8), pl.ds(base, NB)] for i in range(16)]
    rows = lax.broadcasted_iota(jnp.int32, (8, NB), 0)
    lanes = lax.broadcasted_iota(jnp.int32, (8, NB), 1)
    Z = [jnp.where(rows + 8 * i == lanes, 1.0, 0.0).astype(jnp.float32) for i in range(16)]
    full = lambda x: jnp.broadcast_to(x, (8, NB))
    for t in range(16):
        C = [full(D[t][:, 8 * t + c:8 * t + c + 1]) for c in range(8)]
        X, Y = D[t], Z[t]
        for s in range(8):
            piv = full(C[s][s:s + 1])
            rs = lax.rsqrt(piv)
            xr, yr = full(X[s:s + 1]) * rs, full(Y[s:s + 1]) * rs
            u_ref[8 * t + s:8 * t + s + 1, :] = xr[s:s + 1]
            z_ref[8 * t + s:8 * t + s + 1, :] = yr[s:s + 1]
            inv = rs * rs
            mult = C[s] * inv
            X0, Y0 = full(X[s:s + 1]), full(Y[s:s + 1])
            X = jnp.where(rows == s, X0 * inv, X - mult * X0)
            Y = jnp.where(rows == s, Y0 * inv, Y - mult * Y0)
            for c in range(s + 1, 8):
                c0 = full(C[c][s:s + 1])
                C[c] = jnp.where(rows == s, c0 * inv, C[c] - mult * c0)
        for i in range(t + 1, 16):
            d, z = D[i], Z[i]
            cols = [full(D[i][:, 8 * t + c:8 * t + c + 1]) for c in range(8)]
            for c in range(8):
                d = d - cols[c] * full(X[c:c + 1])
                z = z - cols[c] * full(Y[c:c + 1])
            D[i], Z[i] = d, z


def chol_kernel(scale, g_ref, r_ref, work, u_ref, z_ref):
    size = work.shape[0]
    n = size // NB
    for b, (i, j) in enumerate(tiles(size)):
        work[i * NB:(i + 1) * NB, j * NB:(j + 1) * NB] = g_ref[b * NB:(b + 1) * NB, :] * scale
    for i in range(1, n):
        r_ref[i * NB:(i + 1) * NB, :i * NB] = jnp.zeros((NB, i * NB), jnp.float32)
    tri = lax.broadcasted_iota(jnp.int32, (NB, NB), 0) <= lax.broadcasted_iota(jnp.int32, (NB, NB), 1)

    @pl.loop(0, n)
    def _(j):
        factor(work, j, u_ref, z_ref)
        for jj in range(n):
            @pl.when(j == jj)
            def _(jj=jj):
                lo, hi = jj * NB, (jj + 1) * NB
                r_ref[lo:hi, lo:hi] = jnp.where(tri, u_ref[...], 0.0)
                if jj < n - 1:
                    panel = jnp.dot(z_ref[...], work[lo:hi, hi:], precision=HIGHEST, preferred_element_type=jnp.float32)
                    r_ref[lo:hi, hi:] = panel
                    step = 2 * NB
                    for a in range(hi, size, step):
                        b = min(a + step, size)
                        strip = lax.dot_general(r_ref[lo:hi, a:b], r_ref[lo:hi, a:], (((0,), (0,)), ((), ())), precision=HIGHEST, preferred_element_type=jnp.float32)
                        work[a:b, a:] = work[a:b, a:] - strip


def factored(packed, size, scale):
    return pl.pallas_call(
        functools.partial(chol_kernel, scale),
        out_shape=jax.ShapeDtypeStruct((size, size), jnp.float32),
        in_specs=[pl.BlockSpec(memory_space=pltpu.VMEM)],
        out_specs=pl.BlockSpec(memory_space=pltpu.VMEM),
        scratch_shapes=[pltpu.VMEM((size, size), jnp.float32), pltpu.VMEM((NB, NB), jnp.float32), pltpu.VMEM((NB, NB), jnp.float32)],
        compiler_params=pltpu.CompilerParams(vmem_limit_bytes=56 * 2**20),
    )(packed)


def pack_kernel(fluid, start_ref, place_ref, x_ref, o_ref):
    rows, height, columns = x_ref.shape
    times = o_ref.shape[0]
    width = columns + NB
    o_ref[...] = jnp.zeros_like(o_ref)
    target = lax.broadcasted_iota(jnp.int32, (width, columns), 0)

    @pl.loop(0, rows)
    def _(row):
        x = x_ref[row]
        high = x.astype(jnp.bfloat16).astype(jnp.float32)
        rest = x - high
        middle = rest.astype(jnp.bfloat16).astype(jnp.float32)
        terms = jnp.concatenate([high, middle, rest - middle], 0).astype(jnp.bfloat16)
        choice = jnp.where(place_ref[pl.ds(row, 1), :] == target, 1.0, 0.0).astype(jnp.bfloat16)
        moved = lax.dot_general(terms, choice, (((1,), (1,)), ((), ())), preferred_element_type=jnp.float32)
        moved = moved[:height] + moved[height:2 * height] + moved[2 * height:]
        for part in range(height // times):
            span = pl.ds(pl.multiple_of(part * fluid + start_ref[row] * NB, NB), width)
            o_ref[:, span] += moved[part * times:(part + 1) * times]


def packed_points(stacked, mask):
    quantities, times, rows, columns = stacked.shape
    fluid = columns * (rows + 2) // 2
    order = jnp.arange(columns)
    before = (order[:, None] < order[None, :]).astype(jnp.bfloat16)
    in_row = jnp.dot(mask.astype(jnp.bfloat16), before, preferred_element_type=jnp.float32).astype(jnp.int32)
    filled = jnp.sum(mask, 1)
    ranks = jnp.arange(rows)
    offset = jnp.sum(jnp.where(ranks[None, :] < ranks[:, None], filled[None, :], 0), 1)
    place = jnp.where(mask > 0, in_row + (offset % NB)[:, None], -1)
    by_row = jnp.transpose(stacked, (2, 0, 1, 3)).reshape(rows, quantities * times, columns)
    return pl.pallas_call(
        functools.partial(pack_kernel, fluid),
        out_shape=jax.ShapeDtypeStruct((times, quantities * fluid + columns + NB), jnp.float32),
        in_specs=[pl.BlockSpec(memory_space=pltpu.SMEM), pl.BlockSpec(memory_space=pltpu.VMEM), pl.BlockSpec(memory_space=pltpu.VMEM)],
        out_specs=pl.BlockSpec(memory_space=pltpu.VMEM),
        compiler_params=pltpu.CompilerParams(vmem_limit_bytes=56 * 2**20),
    )(offset // NB, place, by_row), quantities * fluid // NB


def first_chunk(device, chunks, count):
    return device * chunks // count


def exchange_kernel(count, chunks, x_ref, o_ref, send, recv):
    me = lax.axis_index("blk")
    times = x_ref.shape[0]
    least = chunks // count
    most = -(-chunks // count)

    barrier = pltpu.get_barrier_semaphore()

    def greet(step, carry):
        pl.semaphore_signal(barrier, inc=1, device_id={"blk": (me + step) % count}, device_id_type=MESH_ID)
        return carry

    lax.fori_loop(1, count, greet, 0)
    mine = pl.ds(pl.multiple_of(me * times, 8), times)
    o_ref[mine, :] = x_ref[:, pl.ds(pl.multiple_of(first_chunk(me, chunks, count) * NB, NB), most * NB)]
    pl.semaphore_wait(barrier, count - 1)

    def copy(step, number):
        device = (me + step) % count
        first = first_chunk(device, chunks, count)
        return pltpu.make_async_remote_copy(
            src_ref=x_ref.at[:, pl.ds(pl.multiple_of(first * NB, NB), number * NB)],
            dst_ref=o_ref.at[mine, pl.ds(0, number * NB)],
            send_sem=send.at[step - 1], recv_sem=recv.at[step - 1],
            device_id={"blk": device}, device_id_type=MESH_ID)

    def held(device):
        return first_chunk(device + 1, chunks, count) - first_chunk(device, chunks, count)

    def each(step, device, act):
        for number in sorted({least, most}):
            @pl.when(held(device) == number)
            def _(number=number):
                act(copy(step, number))

    def begin(step, carry):
        each(step, (me + step) % count, lambda c: c.start())
        return carry

    def finish(step, carry):
        each(step, me, lambda c: c.wait_recv())
        each(step, (me + step) % count, lambda c: c.wait_send())
        return carry

    lax.fori_loop(1, count, begin, 0)
    lax.fori_loop(1, count, finish, 0)


def exchanged(points, chunks):
    count = lax.axis_size("blk")
    width = -(-chunks // count) * NB
    got = pl.pallas_call(
        functools.partial(exchange_kernel, count, chunks),
        out_shape=jax.ShapeDtypeStruct((points.shape[0] * count, width), jnp.float32),
        in_specs=[pl.BlockSpec(memory_space=pltpu.VMEM)],
        out_specs=pl.BlockSpec(memory_space=pltpu.VMEM),
        scratch_shapes=[pltpu.SemaphoreType.DMA((count - 1,))] * 2,
        compiler_params=pltpu.CompilerParams(collective_id=1, has_side_effects=True, vmem_limit_bytes=56 * 2**20),
    )(points)
    me = lax.axis_index("blk")
    valid = (first_chunk(me + 1, chunks, count) - first_chunk(me, chunks, count)) * NB
    return jnp.where(jnp.arange(width)[None, :] < valid, got, 0.0)


def padded(cells, sides, width):
    for axis, dim in sides:
        count = lax.axis_size(axis)
        head = lax.slice_in_dim(cells, 0, width, axis=dim)
        tail = lax.slice_in_dim(cells, cells.shape[dim] - width, cells.shape[dim], axis=dim)
        cells = jnp.concatenate(
            [
                lax.ppermute(tail, axis, [(i, (i + 1) % count) for i in range(count)]),
                cells,
                lax.ppermute(head, axis, [((i + 1) % count, i) for i in range(count)]),
            ],
            axis=dim,
        )
    return cells


def pair_gram(left_block, right_block):
    return jnp.einsum("tm,sm->ts", left_block, right_block, precision=lax.Precision.HIGH)


def per_device(fields, mask):
    widened = padded(fields[1:3], (("grp", 2),), 1)
    middle = widened[:, :, 1:-1]
    slope_rows = 0.5 * (widened[:, :, 2:] - widened[:, :, :-2])
    slope_cols = 0.5 * (jnp.roll(middle, -1, 3) - jnp.roll(middle, 1, 3))
    active_force = jnp.stack([slope_rows[0] + slope_cols[1], slope_rows[1] - slope_cols[0]])
    stacked = jnp.concatenate([fields, active_force], 0)
    groups = lax.axis_size("grp")
    rows_here, columns = mask.shape
    snapshots = exchanged(*packed_points(stacked, mask))
    packed = summed(pair_gram(snapshots, snapshots))
    if groups > 1:
        packed = lax.psum(packed, "grp")
    r_factor = factored(packed, snapshots.shape[0], 1.0 / float(rows_here * groups * columns))
    return (r_factor, active_force)


def solution(mesh):
    placed = (P(None, "blk", "grp", None), P("grp", None))
    return jax.shard_map(
        per_device,
        mesh=mesh,
        in_specs=placed,
        out_specs=(P(), P(None, "blk", "grp", None)),
        check_vma=False,
    )
```

```python
import functools
import jax
import jax.numpy as jnp
from jax import lax
from jax.experimental import pallas as pl
from jax.experimental.pallas import tpu as pltpu
from jax.sharding import PartitionSpec as P

NB = 128
HIGHEST = lax.Precision.HIGHEST
MESH_ID = pl.DeviceIdType.MESH


def tiles(size):
    n = size // NB
    return [(i, j) for i in range(n) for j in range(i, n)]


def packed_rows(size, count):
    unit = 8 * count
    return -(-len(tiles(size)) * NB // unit) * unit


def stages(count):
    return [(1, 2), (2, 4), (8, count // 8)]


def sum_kernel(count, g_ref, full, acc, buf0, buf1, buf2, send, recv, gsend, grecv):
    me = lax.axis_index("blk")
    plan = stages(count)
    bufs = [buf0, buf1, buf2]

    def peer(stride, size, step):
        here = (me // stride) % size
        there = (here + step) % size
        return there, me + (there - here) * stride

    barrier = pltpu.get_barrier_semaphore()
    greeted = 0
    for stride, size in plan:
        for step in range(1, size):
            pl.semaphore_signal(barrier, inc=1, device_id={"blk": peer(stride, size, step)[1]}, device_id_type=MESH_ID)
            greeted += 1
    pl.semaphore_wait(barrier, greeted)

    started = []
    base = 0
    length = g_ref.shape[0]
    source = g_ref
    slot = 0
    owned = []
    for (stride, size), buf in zip(plan, bufs):
        length = length // size
        here = (me // stride) % size
        wave = []
        for step in range(1, size):
            there, device = peer(stride, size, step)
            copy = pltpu.make_async_remote_copy(
                src_ref=source.at[pl.ds(pl.multiple_of(base + there * length, 8), length)],
                dst_ref=buf.at[step - 1],
                send_sem=send.at[slot], recv_sem=recv.at[slot],
                device_id={"blk": device}, device_id_type=MESH_ID)
            copy.start()
            wave.append(copy)
            slot += 1
        base = pl.multiple_of(base + here * length, 8)
        value = source[pl.ds(base, length), :]
        for step, copy in enumerate(wave):
            copy.wait_recv()
            value = value + buf[step]
        acc[pl.ds(base, length), :] = value
        source = acc
        owned.append((base, length))
        started += wave
    full[pl.ds(base, length), :] = acc[pl.ds(base, length), :]
    slot = 0
    for (stride, size), (base, length) in reversed(list(zip(plan, owned))):
        piece = pl.ds(base, length)
        wave = []
        for step in range(1, size):
            copy = pltpu.make_async_remote_copy(
                src_ref=full.at[piece], dst_ref=full.at[piece],
                send_sem=gsend.at[slot], recv_sem=grecv.at[slot],
                device_id={"blk": peer(stride, size, step)[1]}, device_id_type=MESH_ID)
            copy.start()
            wave.append(copy)
            slot += 1
        for copy in wave:
            copy.wait_recv()
        started += wave
    for copy in started:
        copy.wait_send()


def summed(gram):
    count = lax.axis_size("blk")
    total = gram.shape[0]
    plan = stages(count)
    lengths = [total // 2, total // 8, total // count]
    copies = sum(s - 1 for _, s in plan)
    return pl.pallas_call(
        functools.partial(sum_kernel, count),
        out_shape=jax.ShapeDtypeStruct((total, NB), jnp.float32),
        in_specs=[pl.BlockSpec(memory_space=pltpu.VMEM)],
        out_specs=pl.BlockSpec(memory_space=pltpu.VMEM),
        scratch_shapes=[pltpu.VMEM((total, NB), jnp.float32)]
        + [pltpu.VMEM((s - 1, rows, NB), jnp.float32) for (_, s), rows in zip(plan, lengths)]
        + [pltpu.SemaphoreType.DMA((copies,))] * 4,
        compiler_params=pltpu.CompilerParams(collective_id=0, has_side_effects=True, vmem_limit_bytes=56 * 2**20),
    )(gram)


def factor(work, j, u_ref, z_ref):
    base = pl.multiple_of(j * NB, NB)
    D = [work[pl.ds(base + 8 * i, 8), pl.ds(base, NB)] for i in range(16)]
    rows = lax.broadcasted_iota(jnp.int32, (8, NB), 0)
    lanes = lax.broadcasted_iota(jnp.int32, (8, NB), 1)
    Z = [jnp.where(rows + 8 * i == lanes, 1.0, 0.0).astype(jnp.float32) for i in range(16)]
    full = lambda x: jnp.broadcast_to(x, (8, NB))
    for t in range(16):
        C = [full(D[t][:, 8 * t + c:8 * t + c + 1]) for c in range(8)]
        X, Y = D[t], Z[t]
        for s in range(8):
            piv = full(C[s][s:s + 1])
            rs = lax.rsqrt(piv)
            xr, yr = full(X[s:s + 1]) * rs, full(Y[s:s + 1]) * rs
            u_ref[8 * t + s:8 * t + s + 1, :] = xr[s:s + 1]
            z_ref[8 * t + s:8 * t + s + 1, :] = yr[s:s + 1]
            inv = rs * rs
            mult = C[s] * inv
            X0, Y0 = full(X[s:s + 1]), full(Y[s:s + 1])
            X = jnp.where(rows == s, X0 * inv, X - mult * X0)
            Y = jnp.where(rows == s, Y0 * inv, Y - mult * Y0)
            for c in range(s + 1, 8):
                c0 = full(C[c][s:s + 1])
                C[c] = jnp.where(rows == s, c0 * inv, C[c] - mult * c0)
        for i in range(t + 1, 16):
            d, z = D[i], Z[i]
            cols = [full(D[i][:, 8 * t + c:8 * t + c + 1]) for c in range(8)]
            for c in range(8):
                d = d - cols[c] * full(X[c:c + 1])
                z = z - cols[c] * full(Y[c:c + 1])
            D[i], Z[i] = d, z


def chol_kernel(scale, g_ref, r_ref, work, u_ref, z_ref):
    size = work.shape[0]
    n = size // NB
    for b, (i, j) in enumerate(tiles(size)):
        work[i * NB:(i + 1) * NB, j * NB:(j + 1) * NB] = g_ref[b * NB:(b + 1) * NB, :] * scale
    for i in range(1, n):
        r_ref[i * NB:(i + 1) * NB, :i * NB] = jnp.zeros((NB, i * NB), jnp.float32)
    tri = lax.broadcasted_iota(jnp.int32, (NB, NB), 0) <= lax.broadcasted_iota(jnp.int32, (NB, NB), 1)

    @pl.loop(0, n)
    def _(j):
        factor(work, j, u_ref, z_ref)
        for jj in range(n):
            @pl.when(j == jj)
            def _(jj=jj):
                lo, hi = jj * NB, (jj + 1) * NB
                r_ref[lo:hi, lo:hi] = jnp.where(tri, u_ref[...], 0.0)
                if jj < n - 1:
                    panel = jnp.dot(z_ref[...], work[lo:hi, hi:], precision=HIGHEST, preferred_element_type=jnp.float32)
                    r_ref[lo:hi, hi:] = panel
                    step = 2 * NB
                    for a in range(hi, size, step):
                        b = min(a + step, size)
                        strip = lax.dot_general(r_ref[lo:hi, a:b], r_ref[lo:hi, a:], (((0,), (0,)), ((), ())), precision=HIGHEST, preferred_element_type=jnp.float32)
                        work[a:b, a:] = work[a:b, a:] - strip


def factored(packed, size, scale):
    return pl.pallas_call(
        functools.partial(chol_kernel, scale),
        out_shape=jax.ShapeDtypeStruct((size, size), jnp.float32),
        in_specs=[pl.BlockSpec(memory_space=pltpu.VMEM)],
        out_specs=pl.BlockSpec(memory_space=pltpu.VMEM),
        scratch_shapes=[pltpu.VMEM((size, size), jnp.float32), pltpu.VMEM((NB, NB), jnp.float32), pltpu.VMEM((NB, NB), jnp.float32)],
        compiler_params=pltpu.CompilerParams(vmem_limit_bytes=56 * 2**20),
    )(packed)


def pack_kernel(fluid, x_ref, above_ref, below_ref, mask_ref, o_ref, force_ref, rank_ref, *halves):
    rows, columns = mask_ref.shape
    times = o_ref.shape[0]
    width = columns + NB
    o_ref[...] = jnp.zeros_like(o_ref)
    cells, forces = halves[:columns // NB], halves[columns // NB:]
    for h, half in enumerate(cells):
        half[...] = x_ref[:, h * NB:(h + 1) * NB]
    target = lax.broadcasted_iota(jnp.int32, (width, columns), 0)
    before = lax.broadcasted_iota(jnp.int32, (columns, columns), 0) < lax.broadcasted_iota(jnp.int32, (columns, columns), 1)
    ones = jnp.where(mask_ref[...] > 0, 1.0, 0.0)
    rank_ref[...] = jnp.dot(
        ones.astype(jnp.bfloat16), jnp.where(before, 1.0, 0.0).astype(jnp.bfloat16), preferred_element_type=jnp.float32
    ).astype(jnp.int32)

    def load(quantity, row):
        span = pl.ds(quantity * times * rows + row, times, stride=rows)
        return jnp.concatenate([half[span, :] for half in cells], 1)

    def side_slope(values):
        return 0.5 * (pltpu.roll(values, columns - 1, 1) - pltpu.roll(values, 1, 1))

    def step(row, filled):
        slopes = []
        here = [load(quantity, row) for quantity in range(3)]
        for q in range(2):
            span = slice(q * times, (q + 1) * times)
            upper = jnp.where(row == 0, above_ref[span, :], load(q + 1, jnp.maximum(row - 1, 0)))
            lower = jnp.where(row == rows - 1, below_ref[span, :], load(q + 1, jnp.minimum(row + 1, rows - 1)))
            slopes.append(0.5 * (lower - upper))
        force_x = slopes[0] + side_slope(here[2])
        force_y = slopes[1] - side_slope(here[1])
        for h, half in enumerate(forces):
            half[pl.ds(row, times, stride=rows), :] = force_x[:, h * NB:(h + 1) * NB]
            half[pl.ds(times * rows + row, times, stride=rows), :] = force_y[:, h * NB:(h + 1) * NB]
        x = jnp.concatenate(here + [force_x, force_y], 0)
        height = 5 * times
        high = x.astype(jnp.bfloat16).astype(jnp.float32)
        rest = x - high
        middle = rest.astype(jnp.bfloat16).astype(jnp.float32)
        terms = jnp.concatenate([high, middle, rest - middle], 0).astype(jnp.bfloat16)
        open_row = mask_ref[pl.ds(row, 1), :] > 0
        place = jnp.where(open_row, rank_ref[pl.ds(row, 1), :] + lax.rem(filled, NB), -1)
        choice = jnp.where(place == target, 1.0, 0.0).astype(jnp.bfloat16)
        moved = lax.dot_general(terms, choice, (((1,), (1,)), ((), ())), preferred_element_type=jnp.float32)
        moved = moved[:height] + moved[height:2 * height] + moved[2 * height:]
        start = lax.div(filled, NB) * NB
        for part in range(5):
            span = pl.ds(pl.multiple_of(part * fluid + start, NB), width)
            o_ref[:, span] += moved[part * times:(part + 1) * times]
        return filled + jnp.sum(jnp.where(open_row, 1.0, 0.0)).astype(jnp.int32)

    lax.fori_loop(0, rows, step, jnp.int32(0))
    for h, half in enumerate(forces):
        force_ref[:, h * NB:(h + 1) * NB] = half[...]


def packed_points(fields, above, below, mask):
    quantities, times, rows, columns = fields.shape
    fluid = columns * (rows + 2) // 2
    points, force = pl.pallas_call(
        functools.partial(pack_kernel, fluid),
        out_shape=(
            jax.ShapeDtypeStruct((times, 5 * fluid + columns + NB), jnp.float32),
            jax.ShapeDtypeStruct((2 * times * rows, columns), jnp.float32),
        ),
        in_specs=[pl.BlockSpec(memory_space=pltpu.VMEM)] * 4,
        out_specs=(pl.BlockSpec(memory_space=pltpu.VMEM),) * 2,
        scratch_shapes=[pltpu.VMEM((rows, columns), jnp.int32)]
        + [pltpu.VMEM((3 * times * rows, NB), jnp.float32)] * (columns // NB)
        + [pltpu.VMEM((2 * times * rows, NB), jnp.float32)] * (columns // NB),
        compiler_params=pltpu.CompilerParams(vmem_limit_bytes=56 * 2**20),
    )(fields.reshape(-1, columns), above.reshape(-1, columns), below.reshape(-1, columns), mask)
    return points, 5 * fluid // NB, force.reshape(2, times, rows, columns)


def first_chunk(device, chunks, count):
    return device * chunks // count


def exchange_kernel(count, chunks, x_ref, o_ref, send, recv):
    me = lax.axis_index("blk")
    times = x_ref.shape[0]
    least = chunks // count
    most = -(-chunks // count)

    barrier = pltpu.get_barrier_semaphore()

    def greet(step, carry):
        pl.semaphore_signal(barrier, inc=1, device_id={"blk": (me + step) % count}, device_id_type=MESH_ID)
        return carry

    lax.fori_loop(1, count, greet, 0)
    mine = pl.ds(pl.multiple_of(me * times, 8), times)
    o_ref[mine, :] = x_ref[:, pl.ds(pl.multiple_of(first_chunk(me, chunks, count) * NB, NB), most * NB)]
    pl.semaphore_wait(barrier, count - 1)

    def copy(step, number):
        device = (me + step) % count
        first = first_chunk(device, chunks, count)
        return pltpu.make_async_remote_copy(
            src_ref=x_ref.at[:, pl.ds(pl.multiple_of(first * NB, NB), number * NB)],
            dst_ref=o_ref.at[mine, pl.ds(0, number * NB)],
            send_sem=send.at[step - 1], recv_sem=recv.at[step - 1],
            device_id={"blk": device}, device_id_type=MESH_ID)

    def held(device):
        return first_chunk(device + 1, chunks, count) - first_chunk(device, chunks, count)

    def each(step, device, act):
        for number in sorted({least, most}):
            @pl.when(held(device) == number)
            def _(number=number):
                act(copy(step, number))

    def begin(step, carry):
        each(step, (me + step) % count, lambda c: c.start())
        return carry

    def finish(step, carry):
        each(step, me, lambda c: c.wait_recv())
        each(step, (me + step) % count, lambda c: c.wait_send())
        return carry

    lax.fori_loop(1, count, begin, 0)
    lax.fori_loop(1, count, finish, 0)


def exchanged(points, chunks):
    count = lax.axis_size("blk")
    width = -(-chunks // count) * NB
    return pl.pallas_call(
        functools.partial(exchange_kernel, count, chunks),
        out_shape=jax.ShapeDtypeStruct((points.shape[0] * count, width), jnp.float32),
        in_specs=[pl.BlockSpec(memory_space=pltpu.VMEM)],
        out_specs=pl.BlockSpec(memory_space=pltpu.VMEM),
        scratch_shapes=[pltpu.SemaphoreType.DMA((count - 1,))] * 2,
        compiler_params=pltpu.CompilerParams(collective_id=1, has_side_effects=True, vmem_limit_bytes=56 * 2**20),
    )(points)


def gram_kernel(count, chunks, x_ref, g_ref, high_ref, low_ref):
    size, width = x_ref.shape
    me = lax.axis_index("blk")
    valid = (first_chunk(me + 1, chunks, count) - first_chunk(me, chunks, count)) * NB
    x = jnp.where(lax.broadcasted_iota(jnp.int32, (size, width), 1) < valid, x_ref[...], 0.0)
    high_ref[...] = x.astype(jnp.bfloat16)
    low_ref[...] = (x - x.astype(jnp.bfloat16).astype(jnp.float32)).astype(jnp.bfloat16)

    def times(left, right):
        return lax.dot_general(left, right, (((1,), (1,)), ((), ())), preferred_element_type=jnp.float32)

    b = 0
    for i in range(size // NB):
        rows = slice(i * NB, (i + 1) * NB)
        strip = times(high_ref[rows, :], high_ref[i * NB:, :])
        strip = strip + times(high_ref[rows, :], low_ref[i * NB:, :])
        strip = strip + times(low_ref[rows, :], high_ref[i * NB:, :])
        for j in range(size // NB - i):
            g_ref[b * NB:(b + 1) * NB, :] = strip[:, j * NB:(j + 1) * NB]
            b += 1
    if b * NB < g_ref.shape[0]:
        g_ref[b * NB:, :] = jnp.zeros((g_ref.shape[0] - b * NB, NB), jnp.float32)


def upper_gram(snapshots, chunks):
    count = lax.axis_size("blk")
    return pl.pallas_call(
        functools.partial(gram_kernel, count, chunks),
        out_shape=jax.ShapeDtypeStruct((packed_rows(snapshots.shape[0], count), NB), jnp.float32),
        in_specs=[pl.BlockSpec(memory_space=pltpu.VMEM)],
        out_specs=pl.BlockSpec(memory_space=pltpu.VMEM),
        scratch_shapes=[pltpu.VMEM(snapshots.shape, jnp.bfloat16)] * 2,
        compiler_params=pltpu.CompilerParams(vmem_limit_bytes=56 * 2**20),
    )(snapshots)


def row_edges(cells):
    count = lax.axis_size("grp")
    head, tail = cells[:, :, 0], cells[:, :, -1]
    if count == 1:
        return tail, head
    return (
        lax.ppermute(tail, "grp", [(i, (i + 1) % count) for i in range(count)]),
        lax.ppermute(head, "grp", [((i + 1) % count, i) for i in range(count)]),
    )


def per_device(fields, mask):
    above, below = row_edges(fields[1:3])
    groups = lax.axis_size("grp")
    rows_here, columns = mask.shape
    points, chunks, active_force = packed_points(fields, above, below, mask)
    snapshots = exchanged(points, chunks)
    size = snapshots.shape[0]
    packed = summed(upper_gram(snapshots, chunks))
    if groups > 1:
        packed = lax.psum(packed, "grp")
    r_factor = factored(packed, size, 1.0 / float(rows_here * groups * columns))
    return (r_factor, active_force)


def solution(mesh):
    placed = (P(None, "blk", "grp", None), P("grp", None))
    return jax.shard_map(
        per_device,
        mesh=mesh,
        in_specs=placed,
        out_specs=(P(), P(None, "blk", "grp", None)),
        check_vma=False,
    )
```

```python
import functools
import jax
import jax.numpy as jnp
from jax import lax
from jax.experimental import pallas as pl
from jax.experimental.pallas import tpu as pltpu
from jax.sharding import PartitionSpec as P

NB = 128
PARTS = 2
HIGHEST = lax.Precision.HIGHEST
MESH_ID = pl.DeviceIdType.MESH


def tiles(size):
    n = size // NB
    return [(i, j) for i in range(n) for j in range(i, n)]


def packed_rows(size, count):
    unit = 8 * count * PARTS
    return -(-len(tiles(size)) * NB // unit) * unit


def stages(count):
    return [(1, 2), (2, 4), (8, count // 8)]


def sum_kernel(count, g_ref, full, acc, buf0, buf1, buf2, send, recv, gsend, grecv):
    me = lax.axis_index("blk")
    plan = stages(count)
    bufs = [buf0, buf1, buf2]

    def peer(stride, size, step):
        here = (me // stride) % size
        there = (here + step) % size
        return there, me + (there - here) * stride

    barrier = pltpu.get_barrier_semaphore()
    greeted = 0
    for stride, size in plan:
        for step in range(1, size):
            pl.semaphore_signal(barrier, inc=1, device_id={"blk": peer(stride, size, step)[1]}, device_id_type=MESH_ID)
            greeted += 1
    pl.semaphore_wait(barrier, greeted)

    started = []
    part = g_ref.shape[0] // PARTS
    copies = sum(size - 1 for _, size in plan)
    state = [dict(base=half * part, length=part, source=g_ref, owned=[]) for half in range(PARTS)]
    slots = [sum(size - 1 for _, size in plan[:k]) for k in range(len(plan))]

    def scatter_begin(half, k):
        at = state[half]
        stride, size = plan[k]
        at["length"] //= size
        at["wave"] = []
        for step in range(1, size):
            there, device = peer(stride, size, step)
            slot = half * copies + slots[k] + step - 1
            copy = pltpu.make_async_remote_copy(
                src_ref=at["source"].at[pl.ds(pl.multiple_of(at["base"] + there * at["length"], 8), at["length"])],
                dst_ref=bufs[k].at[half * (size - 1) + step - 1],
                send_sem=send.at[slot], recv_sem=recv.at[slot],
                device_id={"blk": device}, device_id_type=MESH_ID)
            copy.start()
            at["wave"].append(copy)

    def scatter_end(half, k):
        at = state[half]
        stride, size = plan[k]
        at["base"] = pl.multiple_of(at["base"] + ((me // stride) % size) * at["length"], 8)
        piece = pl.ds(at["base"], at["length"])
        value = at["source"][piece, :]
        for step, copy in enumerate(at["wave"]):
            copy.wait_recv()
            value = value + bufs[k][half * (size - 1) + step]
        target = acc if k < len(plan) - 1 else full
        target[piece, :] = value
        at["source"] = acc
        at["owned"].append(piece)
        started.extend(at["wave"])

    def gather_begin(half, k):
        at = state[half]
        stride, size = plan[k]
        piece = at["owned"][k]
        at["wave"] = []
        for step in range(1, size):
            slot = half * copies + slots[k] + step - 1
            copy = pltpu.make_async_remote_copy(
                src_ref=full.at[piece], dst_ref=full.at[piece],
                send_sem=gsend.at[slot], recv_sem=grecv.at[slot],
                device_id={"blk": peer(stride, size, step)[1]}, device_id_type=MESH_ID)
            copy.start()
            at["wave"].append(copy)

    def gather_end(half, k):
        for copy in state[half]["wave"]:
            copy.wait_recv()
        started.extend(state[half]["wave"])

    last = len(plan) - 1
    todo = [(scatter_begin, scatter_end, k) for k in range(last + 1)]
    todo += [(gather_begin, gather_end, k) for k in range(last, -1, -1)]
    for half in range(PARTS):
        todo[0][0](half, todo[0][2])
    for now, (_, end, k) in enumerate(todo):
        for half in range(PARTS):
            end(half, k)
            if now + 1 < len(todo):
                todo[now + 1][0](half, todo[now + 1][2])
    for copy in started:
        copy.wait_send()


def summed(gram):
    count = lax.axis_size("blk")
    total = gram.shape[0]
    plan = stages(count)
    lengths = [total // 2 // PARTS, total // 8 // PARTS, total // count // PARTS]
    copies = sum(s - 1 for _, s in plan)
    return pl.pallas_call(
        functools.partial(sum_kernel, count),
        out_shape=jax.ShapeDtypeStruct((total, NB), jnp.float32),
        in_specs=[pl.BlockSpec(memory_space=pltpu.VMEM)],
        out_specs=pl.BlockSpec(memory_space=pltpu.VMEM),
        scratch_shapes=[pltpu.VMEM((total, NB), jnp.float32)]
        + [pltpu.VMEM(((s - 1) * PARTS, rows, NB), jnp.float32) for (_, s), rows in zip(plan, lengths)]
        + [pltpu.SemaphoreType.DMA((copies * PARTS,))] * 4,
        compiler_params=pltpu.CompilerParams(collective_id=0, has_side_effects=True, vmem_limit_bytes=56 * 2**20),
    )(gram)


def factor(work, j, u_ref, z_ref):
    base = pl.multiple_of(j * NB, NB)
    D = [work[pl.ds(base + 8 * i, 8), pl.ds(base, NB)] for i in range(16)]
    rows = lax.broadcasted_iota(jnp.int32, (8, NB), 0)
    lanes = lax.broadcasted_iota(jnp.int32, (8, NB), 1)
    Z = [jnp.where(rows + 8 * i == lanes, 1.0, 0.0).astype(jnp.float32) for i in range(16)]
    full = lambda x: jnp.broadcast_to(x, (8, NB))
    for t in range(16):
        C = [full(D[t][:, 8 * t + c:8 * t + c + 1]) for c in range(8)]
        X, Y = D[t], Z[t]
        for s in range(8):
            piv = full(C[s][s:s + 1])
            rs = lax.rsqrt(piv)
            xr, yr = full(X[s:s + 1]) * rs, full(Y[s:s + 1]) * rs
            u_ref[8 * t + s:8 * t + s + 1, :] = xr[s:s + 1]
            z_ref[8 * t + s:8 * t + s + 1, :] = yr[s:s + 1]
            inv = rs * rs
            mult = C[s] * inv
            X0, Y0 = full(X[s:s + 1]), full(Y[s:s + 1])
            X = jnp.where(rows == s, X0 * inv, X - mult * X0)
            Y = jnp.where(rows == s, Y0 * inv, Y - mult * Y0)
            for c in range(s + 1, 8):
                c0 = full(C[c][s:s + 1])
                C[c] = jnp.where(rows == s, c0 * inv, C[c] - mult * c0)
        for i in range(t + 1, 16):
            d, z = D[i], Z[i]
            cols = [full(D[i][:, 8 * t + c:8 * t + c + 1]) for c in range(8)]
            for c in range(8):
                d = d - cols[c] * full(X[c:c + 1])
                z = z - cols[c] * full(Y[c:c + 1])
            D[i], Z[i] = d, z


def chol_kernel(scale, g_ref, r_ref, work, u_ref, z_ref):
    size = work.shape[0]
    n = size // NB
    for b, (i, j) in enumerate(tiles(size)):
        work[i * NB:(i + 1) * NB, j * NB:(j + 1) * NB] = g_ref[b * NB:(b + 1) * NB, :] * scale
    for i in range(1, n):
        r_ref[i * NB:(i + 1) * NB, :i * NB] = jnp.zeros((NB, i * NB), jnp.float32)
    tri = lax.broadcasted_iota(jnp.int32, (NB, NB), 0) <= lax.broadcasted_iota(jnp.int32, (NB, NB), 1)

    @pl.loop(0, n)
    def _(j):
        factor(work, j, u_ref, z_ref)
        for jj in range(n):
            @pl.when(j == jj)
            def _(jj=jj):
                lo, hi = jj * NB, (jj + 1) * NB
                r_ref[lo:hi, lo:hi] = jnp.where(tri, u_ref[...], 0.0)
                if jj < n - 1:
                    panel = jnp.dot(z_ref[...], work[lo:hi, hi:], precision=HIGHEST, preferred_element_type=jnp.float32)
                    r_ref[lo:hi, hi:] = panel
                    step = 2 * NB
                    for a in range(hi, size, step):
                        b = min(a + step, size)
                        strip = lax.dot_general(r_ref[lo:hi, a:b], r_ref[lo:hi, a:], (((0,), (0,)), ((), ())), precision=HIGHEST, preferred_element_type=jnp.float32)
                        work[a:b, a:] = work[a:b, a:] - strip


def factored(packed, size, scale):
    return pl.pallas_call(
        functools.partial(chol_kernel, scale),
        out_shape=jax.ShapeDtypeStruct((size, size), jnp.float32),
        in_specs=[pl.BlockSpec(memory_space=pltpu.VMEM)],
        out_specs=pl.BlockSpec(memory_space=pltpu.VMEM),
        scratch_shapes=[pltpu.VMEM((size, size), jnp.float32), pltpu.VMEM((NB, NB), jnp.float32), pltpu.VMEM((NB, NB), jnp.float32)],
        compiler_params=pltpu.CompilerParams(vmem_limit_bytes=56 * 2**20),
    )(packed)


def pack_kernel(fluid, x_ref, above_ref, below_ref, mask_ref, o_ref, force_ref, rank_ref, *halves):
    rows, columns = mask_ref.shape
    times = o_ref.shape[0]
    width = columns + NB
    o_ref[...] = jnp.zeros_like(o_ref)
    cells, forces = halves[:columns // NB], halves[columns // NB:]
    for h, half in enumerate(cells):
        half[...] = x_ref[:, h * NB:(h + 1) * NB]
    target = lax.broadcasted_iota(jnp.int32, (width, columns), 0)
    before = lax.broadcasted_iota(jnp.int32, (columns, columns), 0) < lax.broadcasted_iota(jnp.int32, (columns, columns), 1)
    ones = jnp.where(mask_ref[...] > 0, 1.0, 0.0)
    rank_ref[...] = jnp.dot(
        ones.astype(jnp.bfloat16), jnp.where(before, 1.0, 0.0).astype(jnp.bfloat16), preferred_element_type=jnp.float32
    ).astype(jnp.int32)

    def load(quantity, row):
        span = pl.ds(quantity * times * rows + row, times, stride=rows)
        return jnp.concatenate([half[span, :] for half in cells], 1)

    def side_slope(values):
        return 0.5 * (pltpu.roll(values, columns - 1, 1) - pltpu.roll(values, 1, 1))

    def step(row, filled):
        slopes = []
        here = [load(quantity, row) for quantity in range(3)]
        for q in range(2):
            span = slice(q * times, (q + 1) * times)
            upper = jnp.where(row == 0, above_ref[span, :], load(q + 1, jnp.maximum(row - 1, 0)))
            lower = jnp.where(row == rows - 1, below_ref[span, :], load(q + 1, jnp.minimum(row + 1, rows - 1)))
            slopes.append(0.5 * (lower - upper))
        force_x = slopes[0] + side_slope(here[2])
        force_y = slopes[1] - side_slope(here[1])
        for h, half in enumerate(forces):
            half[pl.ds(row, times, stride=rows), :] = force_x[:, h * NB:(h + 1) * NB]
            half[pl.ds(times * rows + row, times, stride=rows), :] = force_y[:, h * NB:(h + 1) * NB]
        x = jnp.concatenate(here + [force_x, force_y], 0)
        height = 5 * times
        high = x.astype(jnp.bfloat16).astype(jnp.float32)
        rest = x - high
        middle = rest.astype(jnp.bfloat16).astype(jnp.float32)
        terms = jnp.concatenate([high, middle, rest - middle], 0).astype(jnp.bfloat16)
        open_row = mask_ref[pl.ds(row, 1), :] > 0
        place = jnp.where(open_row, rank_ref[pl.ds(row, 1), :] + lax.rem(filled, NB), -1)
        choice = jnp.where(place == target, 1.0, 0.0).astype(jnp.bfloat16)
        moved = lax.dot_general(terms, choice, (((1,), (1,)), ((), ())), preferred_element_type=jnp.float32)
        moved = moved[:height] + moved[height:2 * height] + moved[2 * height:]
        start = lax.div(filled, NB) * NB
        for part in range(5):
            span = pl.ds(pl.multiple_of(part * fluid + start, NB), width)
            o_ref[:, span] += moved[part * times:(part + 1) * times]
        return filled + jnp.sum(jnp.where(open_row, 1.0, 0.0)).astype(jnp.int32)

    lax.fori_loop(0, rows, step, jnp.int32(0))
    for h, half in enumerate(forces):
        force_ref[:, h * NB:(h + 1) * NB] = half[...]


def packed_points(fields, above, below, mask):
    quantities, times, rows, columns = fields.shape
    fluid = columns * (rows + 2) // 2
    points, force = pl.pallas_call(
        functools.partial(pack_kernel, fluid),
        out_shape=(
            jax.ShapeDtypeStruct((times, 5 * fluid + columns + NB), jnp.float32),
            jax.ShapeDtypeStruct((2 * times * rows, columns), jnp.float32),
        ),
        in_specs=[pl.BlockSpec(memory_space=pltpu.VMEM)] * 4,
        out_specs=(pl.BlockSpec(memory_space=pltpu.VMEM),) * 2,
        scratch_shapes=[pltpu.VMEM((rows, columns), jnp.int32)]
        + [pltpu.VMEM((3 * times * rows, NB), jnp.float32)] * (columns // NB)
        + [pltpu.VMEM((2 * times * rows, NB), jnp.float32)] * (columns // NB),
        compiler_params=pltpu.CompilerParams(vmem_limit_bytes=56 * 2**20),
    )(fields.reshape(-1, columns), above.reshape(-1, columns), below.reshape(-1, columns), mask)
    return points, 5 * fluid // NB, force.reshape(2, times, rows, columns)


def first_chunk(device, chunks, count):
    return device * chunks // count


def exchange_kernel(count, chunks, x_ref, o_ref, send, recv):
    me = lax.axis_index("blk")
    times = x_ref.shape[0]
    least = chunks // count
    most = -(-chunks // count)

    barrier = pltpu.get_barrier_semaphore()

    def greet(step, carry):
        pl.semaphore_signal(barrier, inc=1, device_id={"blk": (me + step) % count}, device_id_type=MESH_ID)
        return carry

    lax.fori_loop(1, count, greet, 0)
    mine = pl.ds(pl.multiple_of(me * times, 8), times)
    o_ref[mine, :] = x_ref[:, pl.ds(pl.multiple_of(first_chunk(me, chunks, count) * NB, NB), most * NB)]
    pl.semaphore_wait(barrier, count - 1)

    def copy(step, number):
        device = (me + step) % count
        first = first_chunk(device, chunks, count)
        return pltpu.make_async_remote_copy(
            src_ref=x_ref.at[:, pl.ds(pl.multiple_of(first * NB, NB), number * NB)],
            dst_ref=o_ref.at[mine, pl.ds(0, number * NB)],
            send_sem=send.at[step - 1], recv_sem=recv.at[step - 1],
            device_id={"blk": device}, device_id_type=MESH_ID)

    def held(device):
        return first_chunk(device + 1, chunks, count) - first_chunk(device, chunks, count)

    def each(step, device, act):
        for number in sorted({least, most}):
            @pl.when(held(device) == number)
            def _(number=number):
                act(copy(step, number))

    def begin(step, carry):
        each(step, (me + step) % count, lambda c: c.start())
        return carry

    def finish(step, carry):
        each(step, me, lambda c: c.wait_recv())
        each(step, (me + step) % count, lambda c: c.wait_send())
        return carry

    lax.fori_loop(1, count, begin, 0)
    lax.fori_loop(1, count, finish, 0)


def exchanged(points, chunks):
    count = lax.axis_size("blk")
    width = -(-chunks // count) * NB
    return pl.pallas_call(
        functools.partial(exchange_kernel, count, chunks),
        out_shape=jax.ShapeDtypeStruct((points.shape[0] * count, width), jnp.float32),
        in_specs=[pl.BlockSpec(memory_space=pltpu.VMEM)],
        out_specs=pl.BlockSpec(memory_space=pltpu.VMEM),
        scratch_shapes=[pltpu.SemaphoreType.DMA((count - 1,))] * 2,
        compiler_params=pltpu.CompilerParams(collective_id=1, has_side_effects=True, vmem_limit_bytes=56 * 2**20),
    )(points)


def gram_kernel(count, chunks, x_ref, g_ref, high_ref, low_ref):
    size, width = x_ref.shape
    me = lax.axis_index("blk")
    valid = (first_chunk(me + 1, chunks, count) - first_chunk(me, chunks, count)) * NB
    x = jnp.where(lax.broadcasted_iota(jnp.int32, (size, width), 1) < valid, x_ref[...], 0.0)
    high_ref[...] = x.astype(jnp.bfloat16)
    low_ref[...] = (x - x.astype(jnp.bfloat16).astype(jnp.float32)).astype(jnp.bfloat16)

    def times(left, right):
        return lax.dot_general(left, right, (((1,), (1,)), ((), ())), preferred_element_type=jnp.float32)

    b = 0
    for i in range(size // NB):
        rows = slice(i * NB, (i + 1) * NB)
        strip = times(high_ref[rows, :], high_ref[i * NB:, :])
        strip = strip + times(high_ref[rows, :], low_ref[i * NB:, :])
        strip = strip + times(low_ref[rows, :], high_ref[i * NB:, :])
        for j in range(size // NB - i):
            g_ref[b * NB:(b + 1) * NB, :] = strip[:, j * NB:(j + 1) * NB]
            b += 1
    if b * NB < g_ref.shape[0]:
        g_ref[b * NB:, :] = jnp.zeros((g_ref.shape[0] - b * NB, NB), jnp.float32)


def upper_gram(snapshots, chunks):
    count = lax.axis_size("blk")
    return pl.pallas_call(
        functools.partial(gram_kernel, count, chunks),
        out_shape=jax.ShapeDtypeStruct((packed_rows(snapshots.shape[0], count), NB), jnp.float32),
        in_specs=[pl.BlockSpec(memory_space=pltpu.VMEM)],
        out_specs=pl.BlockSpec(memory_space=pltpu.VMEM),
        scratch_shapes=[pltpu.VMEM(snapshots.shape, jnp.bfloat16)] * 2,
        compiler_params=pltpu.CompilerParams(vmem_limit_bytes=56 * 2**20),
    )(snapshots)


def row_edges(cells):
    count = lax.axis_size("grp")
    head, tail = cells[:, :, 0], cells[:, :, -1]
    if count == 1:
        return tail, head
    return (
        lax.ppermute(tail, "grp", [(i, (i + 1) % count) for i in range(count)]),
        lax.ppermute(head, "grp", [((i + 1) % count, i) for i in range(count)]),
    )


def per_device(fields, mask):
    above, below = row_edges(fields[1:3])
    groups = lax.axis_size("grp")
    rows_here, columns = mask.shape
    points, chunks, active_force = packed_points(fields, above, below, mask)
    snapshots = exchanged(points, chunks)
    size = snapshots.shape[0]
    packed = summed(upper_gram(snapshots, chunks))
    if groups > 1:
        packed = lax.psum(packed, "grp")
    r_factor = factored(packed, size, 1.0 / float(rows_here * groups * columns))
    return (r_factor, active_force)


def solution(mesh):
    placed = (P(None, "blk", "grp", None), P("grp", None))
    return jax.shard_map(
        per_device,
        mesh=mesh,
        in_specs=placed,
        out_specs=(P(), P(None, "blk", "grp", None)),
        check_vma=False,
    )
```
